256 devices in a mesh: section: 16 (over y, x), expert: 4 (over z_lo, core), dp: 4 (over z_hi).
Axes of the slice: x: 4, y: 4, z: 8 (z_hi: 4, z_lo: 2; z = z_hi * 2 + z_lo), core: 2. Of those that a mesh axis runs over, the one named last changes fastest.
Arguments:
- x_now: bfloat16 [16, 2048, 3072], P('section', ('expert', 'dp')), may hold values from -6 to 6
- ids_now: int32 [16, 2048, 4], P('section', ('expert', 'dp')), may hold values from 0 to 15, as said below
- gates_now: float32 [16, 2048, 4], P('section', ('expert', 'dp')), may hold values from 0.05 to 1
- hidden_now: bfloat16 [16, 512, 6144], P('section', ('expert', 'dp')), may hold values from -6 to 6
- x_old: bfloat16 [16, 2048, 3072], P('section', ('expert', 'dp')), may hold values from -6 to 6
- ids_old: int32 [16, 2048, 4], P('section', ('expert', 'dp')), may hold values from 0 to 15, as said below
- gate_grad_old: bfloat16 [16, 512, 6144], P('section', None, ('expert', 'dp')), may hold values from -2 to 2
- up_grad_old: bfloat16 [16, 512, 6144], P('section', None, ('expert', 'dp')), may hold values from -2 to 2
- w_gate: bfloat16 [16, 3072, 6144], P('section', None, ('expert', 'dp')), may hold values from -0.109375 to 0.109375
- w_up: bfloat16 [16, 3072, 6144], P('section', None, ('expert', 'dp')), may hold values from -0.109375 to 0.109375
Outputs:
- passed_grad: bfloat16 [16, 2048, 3072], P('section', ('expert', 'dp'))
- dw_gate: bfloat16 [16, 3072, 6144], P('section', None, ('expert', 'dp'))
- dw_up: bfloat16 [16, 3072, 6144], P('section', None, ('expert', 'dp'))
The draws below stay inside these ranges and needn't reach their ends.
Inputs may be any that keep to these rules, and one draw needn't show every extreme that they name: `ids_now`: each token names 4 different experts. In section s, at most 32 tokens of one aligned block of 128 name expert s mod 16; in every section some block has exactly 32 such tokens, and in some section every block has. `ids_old`: as for ids_now.
All inputs are finite; a program needn't handle non-finite values.
Results may differ from the reference program's by a relative error of at most 0.005.
Values may be sent and summed in bfloat16 or wider, within the bound.
A program may use at most 128 MiB of HBM per device.

```python
import math
import jax
import jax.numpy as jnp
from jax import lax

D = 3072
FF = 6144
EXPERTS = 16
TOP = 4
TOK_DEV = 128
CAP = 32
GROUP = 16
SECTIONS = 16
ROWS = 2048
SLOTS = 512


def routing_lists(key):
    keys = jax.random.split(key, 6)
    blocks = ROWS // TOK_DEV
    expert = (jnp.arange(SECTIONS, dtype=jnp.int32) % EXPERTS)[:, None, None, None]
    counts = jax.random.randint(keys[0], (SECTIONS, blocks), CAP // 2, CAP + 1)
    full_block = jax.random.randint(keys[1], (SECTIONS,), 0, blocks)
    counts = jnp.where(jnp.arange(blocks)[None, :] == full_block[:, None], CAP, counts)
    full_section = jax.random.randint(keys[2], (), 0, SECTIONS)
    counts = jnp.where(jnp.arange(SECTIONS)[:, None] == full_section, CAP, counts)
    scores = jax.random.randint(keys[3], (SECTIONS, blocks, TOK_DEV), 0, 1 << 20) * TOK_DEV + jnp.arange(TOK_DEV, dtype=jnp.int32)
    ranks = jnp.argsort(jnp.argsort(scores, axis=2, stable=True), axis=2, stable=True)
    chosen = ranks < counts[:, :, None]
    other_scores = jax.random.randint(keys[4], (SECTIONS, blocks, TOK_DEV, EXPERTS - 1), 0, 1 << 20) * EXPERTS + jnp.arange(EXPERTS - 1, dtype=jnp.int32)
    picked = lax.top_k(other_scores, TOP)[1].astype(jnp.int32)
    others = jnp.where(picked >= expert, picked + 1, picked)
    position = jax.random.randint(keys[5], (SECTIONS, blocks, TOK_DEV), 0, TOP)
    place = jnp.arange(TOP, dtype=jnp.int32)[None, None, None, :] == position[:, :, :, None]
    ids = jnp.where(chosen[:, :, :, None] & place, expert, others)
    return ids.reshape(SECTIONS, ROWS, TOP).astype(jnp.int32)


def draw_ids_now(key, part):
    key = jax.random.fold_in(key, 11)
    return routing_lists(key)


def draw_ids_old(key, part):
    key = jax.random.fold_in(key, 23)
    return routing_lists(key)


def block_levels(stream_key, shape, cuts, smallest, largest):
    level, own = 1.0, jax.random.fold_in(stream_key, 6)
    for dim, blocks in cuts:
        steps = jnp.exp(jax.random.uniform(jax.random.fold_in(own, dim), (blocks,), jnp.float32, smallest / len(cuts), largest / len(cuts)))
        level = level * jnp.repeat(steps, shape[dim] // blocks).reshape([-1 if axis == dim else 1 for axis in range(len(shape))])
    return level


def gaussian(own_key, extent, scale, reach, cuts=(), kind=jnp.bfloat16):
    entries = jax.random.normal(own_key, extent, jnp.float32) * scale
    if len(cuts) > 0:
        entries = block_levels(own_key, extent, cuts, -0.22, 0.18) * entries
    return jnp.clip(entries, min=-reach, max=reach).astype(kind)


def setup_inputs(seed: int = 0) -> dict:
    arg_keys = jax.random.split(jax.random.key(seed), 11)
    return {
        "x_now": gaussian(arg_keys[0], (SECTIONS, ROWS, D), 1.0, 6.0, ((0, 16), (1, 16))),
        "ids_now": draw_ids_now(jax.random.fold_in(arg_keys[10], 71), 0),
        "gates_now": jnp.clip(jnp.exp(math.log(1.0) - 2.9957323 * jax.random.uniform(arg_keys[2], (SECTIONS, ROWS, TOP), jnp.float32) ** block_levels(arg_keys[2], (SECTIONS, ROWS, TOP), ((0, 16), (1, 16)), -0.2, 0.2)), 0.05, 1.0),
        "hidden_now": gaussian(arg_keys[3], (SECTIONS, SLOTS, FF), 1.0, 6.0, ((0, 16), (1, 16))),
        "x_old": gaussian(arg_keys[4], (SECTIONS, ROWS, D), 1.0, 6.0, ((0, 16), (1, 16))),
        "ids_old": draw_ids_old(jax.random.fold_in(arg_keys[10], 71), 0),
        "gate_grad_old": gaussian(arg_keys[6], (SECTIONS, SLOTS, FF), 0.3, 2.0, ((0, 16), (2, 16))),
        "up_grad_old": gaussian(arg_keys[7], (SECTIONS, SLOTS, FF), 0.3, 2.0, ((0, 16), (2, 16))),
        "w_gate": gaussian(arg_keys[8], (SECTIONS, D, FF), D ** -0.5, 0.109375, ((0, 16), (2, 16))),
        "w_up": gaussian(arg_keys[9], (SECTIONS, D, FF), D ** -0.5, 0.109375, ((0, 16), (2, 16))),
    }


def pack_block(tokens, ids, expert):
    hits = (ids == expert).astype(jnp.int32)
    routed = jnp.sum(hits, axis=1).astype(jnp.int32)
    slot = (jnp.cumsum(routed) - routed).astype(jnp.int32)
    places = jnp.arange(CAP, dtype=jnp.int32)
    table = ((slot[None, :] == places[:, None]) & (routed[None, :] == 1)).astype(jnp.float32)
    packed = jnp.dot(table.astype(jnp.bfloat16), tokens, preferred_element_type=jnp.float32).astype(jnp.bfloat16)
    return table, packed, hits


def one_section(section_args):
    section, x_now, ids_now, gates_now, hidden_now, x_old, ids_old, gate_old, up_old, w_gate, w_up = section_args
    expert = section % EXPERTS
    blocks_x = x_now.reshape(GROUP, TOK_DEV, D)
    blocks_ids = ids_now.reshape(GROUP, TOK_DEV, TOP)
    tables, packed, hits = jax.vmap(pack_block, (0, 0, None))(blocks_x, blocks_ids, expert)
    weight_tok = jnp.sum(gates_now.reshape(GROUP, TOK_DEV, TOP) * hits.astype(jnp.float32), axis=2)
    coef = jnp.sum(tables * weight_tok[:, None, :], axis=2).reshape(SLOTS)
    packed = packed.reshape(SLOTS, D)
    gate = jnp.dot(packed, w_gate, preferred_element_type=jnp.float32)
    up = jnp.dot(packed, w_up, preferred_element_type=jnp.float32)
    sig = jax.nn.sigmoid(gate)
    act = gate * sig
    slope = sig * (1.0 + gate * (1.0 - sig))
    incoming = hidden_now.astype(jnp.float32)
    gate_grad = (incoming * up * slope).astype(jnp.bfloat16)
    up_grad = (incoming * act).astype(jnp.bfloat16)
    dims = (((1,), (1,)), ((), ()))
    summed = lax.dot_general(gate_grad, w_gate, dims, preferred_element_type=jnp.float32)
    summed = summed + lax.dot_general(up_grad, w_up, dims, preferred_element_type=jnp.float32)
    packed_grad = (coef[:, None] * summed).astype(jnp.bfloat16)
    grad_blocks = packed_grad.reshape(GROUP, CAP, D).astype(jnp.float32)
    token_grad = jnp.einsum("gct,gcd->gtd", tables, grad_blocks).astype(jnp.bfloat16).reshape(ROWS, D)
    old_tables, packed_old, old_hits = jax.vmap(pack_block, (0, 0, None))(
        x_old.reshape(GROUP, TOK_DEV, D), ids_old.reshape(GROUP, TOK_DEV, TOP), expert)
    packed_old = packed_old.reshape(SLOTS, D)
    rows_dims = (((0,), (0,)), ((), ()))
    dw_gate = lax.dot_general(packed_old, gate_old, rows_dims, preferred_element_type=jnp.float32).astype(jnp.bfloat16)
    dw_up = lax.dot_general(packed_old, up_old, rows_dims, preferred_element_type=jnp.float32).astype(jnp.bfloat16)
    return token_grad, dw_gate, dw_up


def reference(x_now, ids_now, gates_now, hidden_now, x_old, ids_old, gate_grad_old, up_grad_old, w_gate, w_up):
    sections = jnp.arange(SECTIONS, dtype=jnp.int32)
    token_grads, dw_gate, dw_up = lax.map(one_section, (sections, x_now, ids_now, gates_now, hidden_now, x_old, ids_old, gate_grad_old, up_grad_old, w_gate, w_up))
    tail = jnp.zeros((1, ROWS, D), jnp.bfloat16)
    passed_grad = jnp.concatenate([token_grads[1:], tail], axis=0)
    return passed_grad, dw_gate, dw_up
```

```python
import jax
import jax.numpy as jnp
from jax import lax
from jax.experimental import pallas as pl
from jax.experimental.pallas import tpu as pltpu
from jax.sharding import PartitionSpec as P

EXPERTS = 16
RING = 8
CAP = 32
TOK = 128
D = 3072
WIDTH = 384
BOTH = 2 * WIDTH
LANE = RING * CAP
PIECES = 2
PIECE = D // PIECES
CHUNKS = 4
CHUNK = D // CHUNKS
MESH = pl.DeviceIdType.MESH
F32 = jnp.float32
BF16 = jnp.bfloat16


def routing(ids, expert):
    hits = (ids == expert).astype(F32)
    routed = jnp.sum(hits, axis=0, keepdims=True)
    earlier = lax.broadcasted_iota(jnp.int32, (TOK, TOK), 0) < lax.broadcasted_iota(
        jnp.int32, (TOK, TOK), 1
    )
    counts = jnp.dot(
        jnp.broadcast_to(routed, (16, TOK)).astype(BF16),
        earlier.astype(F32).astype(BF16),
        preferred_element_type=F32,
    )
    slot = counts[0:1].astype(jnp.int32)
    places = lax.broadcasted_iota(jnp.int32, (CAP, TOK), 0)
    table = jnp.where((slot == places) & (routed == 1.0), 1.0, 0.0)
    return table, hits


def kernel(
    ids_now, gates_now, ids_old, x_now, hidden, x_old, gate_old, up_old, w_gate, w_up,
    out, dw_gate, dw_up,
    ids_now_v, gates_now_v, ids_old_v, x_now_v, x_old_v, hid, old, wts, rows_now, rows_old,
    grads, term, send_r, send_l, send_o, land_r, land_l, land_o, tab_out, tab_in,
    load_sem, now_ss, now_rs, old_ss, old_rs, sib_ss, sib_rs, hid_ss, hid_rs, w_ss, w_rs,
    tab_ss, tab_rs, red_ss, red_rs, own_ss, own_rs,
):
    sections = lax.axis_size("section")
    s = lax.axis_index("section")
    e = lax.axis_index("expert")
    z = lax.axis_index("dp") * 2 + e // 2
    k = lax.rem(e, 2)
    expert = lax.rem(s, EXPERTS)

    def chip(by):
        return lax.rem(z + (by + RING), RING)

    def device(by_section, by_z, by_core):
        there = chip(by_z)
        return (
            lax.rem(s + (by_section + sections), sections),
            lax.rem(there, 2) * 2 + lax.rem(k + by_core, 2),
            there // 2,
        )

    def group(there, core):
        return (lax.rem(there, 2) * 2 + core) * 4 + there // 2

    sent = []

    def send(src, dst, ss, rs, to):
        copy = pltpu.make_async_remote_copy(
            src_ref=src, dst_ref=dst, send_sem=ss, recv_sem=rs, device_id=to, device_id_type=MESH
        )
        copy.start()
        sent.append(copy)
        return copy

    barrier = pltpu.get_barrier_semaphore()
    partners = [device(0, by, 0) for by in range(1, RING)] + [device(0, 0, 1)]
    partners += [device(by, dz, 0) for by in (-1, 1) for dz in (-1, 0, 1)]
    for partner in partners:
        pl.semaphore_signal(barrier, inc=1, device_id=partner, device_id_type=MESH)

    loads = 0

    def load(src, dst):
        nonlocal loads
        copy = pltpu.make_async_copy(src, dst, load_sem.at[loads])
        copy.start()
        loads += 1
        return copy

    def columns(start, size, step=128):
        return pl.ds(pl.multiple_of(start, step), size)

    get_now = [load(ids_now, ids_now_v), load(gates_now, gates_now_v), load(x_now, x_now_v)]
    get_old = [load(ids_old, ids_old_v), load(x_old, x_old_v)]
    mine = pl.ds(pl.multiple_of(z * CAP, CAP), CAP)
    gate_place, up_place = columns(k * WIDTH, WIDTH), columns(BOTH + k * WIDTH, WIDTH)
    get_weights = [load(w_gate, wts.at[:, gate_place]), load(w_up, wts.at[:, up_place])]
    get_hidden = [
        load(
            hidden.at[:, columns(group(z, core) * WIDTH, WIDTH)],
            hid.at[mine, core * WIDTH : (core + 1) * WIDTH],
        )
        for core in range(2)
    ]
    get_stored = [load(gate_old, old.at[:, 0:WIDTH]), load(up_old, old.at[:, WIDTH:BOTH])]

    for copy in get_now:
        copy.wait()
    table, hits = routing(ids_now_v[...], expert)
    rows_now[mine, :] = jnp.dot(
        table.astype(BF16), x_now_v[...], preferred_element_type=F32
    ).astype(BF16)
    weight = jnp.sum(gates_now_v[...] * hits, axis=0, keepdims=True)
    coef = jnp.sum(table * weight, axis=1, keepdims=True)
    tab_out[:, 0:TOK] = table
    tab_out[:, TOK : 2 * TOK] = jnp.broadcast_to(coef, (CAP, TOK))

    pl.semaphore_wait(barrier, len(partners))

    def gather_hop(buf, place, ss, rs, hop, waits):
        copies = {}
        for piece in range(PIECES):
            for way, by in enumerate((1, -1)):
                if hop == 3 and (piece < PIECES // 2) != (way == 0):
                    continue
                if waits is not None:
                    waits[way, piece].wait_recv()
                block = buf.at[place(chip(-hop * by)), piece * PIECE : (piece + 1) * PIECE]
                at = (way * 4 + hop) * PIECES + piece
                copies[way, piece] = send(block, block, ss.at[at], rs.at[at], device(0, by, 0))
        return copies

    def now_place(there):
        return pl.ds(pl.multiple_of(there * CAP, CAP), CAP)

    def old_place(there):
        return pl.ds(pl.multiple_of(group(there, k) * CAP, CAP), CAP)

    siblings = []

    def share(by, first=0, last=D):
        block = rows_old.at[old_place(chip(by)), first:last]
        at = len(siblings)
        siblings.append(send(block, block, sib_ss.at[at], sib_rs.at[at], device(0, 0, 1)))

    now_0 = gather_hop(rows_now, now_place, now_ss, now_rs, 0, None)
    hidden_sent = []
    for by in range(1, RING):
        there = chip(by)
        for core in range(2):
            at = (by - 1) * 2 + core
            hidden_sent.append(
                send(
                    hidden.at[:, columns(group(there, core) * WIDTH, WIDTH)],
                    hid.at[mine, core * WIDTH : (core + 1) * WIDTH],
                    hid_ss.at[at],
                    hid_rs.at[at],
                    device(0, by, 0),
                )
            )
    weights_sent = [
        send(w_gate, wts.at[:, gate_place], w_ss.at[0], w_rs.at[0], device(0, 0, 1)),
        send(w_up, wts.at[:, up_place], w_ss.at[1], w_rs.at[1], device(0, 0, 1)),
    ]
    table_sent = send(tab_out, tab_in, tab_ss.at[0], tab_rs.at[0], device(-1, 0, 0))

    for copy in get_old:
        copy.wait()
    old_table, _ = routing(ids_old_v[...], expert)
    rows_old[old_place(z), :] = jnp.dot(
        old_table.astype(BF16), x_old_v[...], preferred_element_type=F32
    ).astype(BF16)

    now_1 = gather_hop(rows_now, now_place, now_ss, now_rs, 1, now_0)
    old_0 = gather_hop(rows_old, old_place, old_ss, old_rs, 0, None)
    share(0)
    now_2 = gather_hop(rows_now, now_place, now_ss, now_rs, 2, now_1)
    now_3 = gather_hop(rows_now, now_place, now_ss, now_rs, 3, now_2)
    old_1 = gather_hop(rows_old, old_place, old_ss, old_rs, 1, old_0)
    share(-1)
    share(1)

    for copy in get_weights + get_hidden + get_stored:
        copy.wait()
    for copy in hidden_sent + weights_sent:
        copy.wait_recv()
    for way in range(2):
        for piece in range(PIECES):
            if (way, piece) not in now_3:
                now_2[way, piece].wait_recv()
    for copy in now_3.values():
        copy.wait_recv()

    def gate_step(j):
        lanes = slice(j * 256, (j + 1) * 256)
        up_lanes = slice(BOTH + j * 256, BOTH + (j + 1) * 256)
        gate = jnp.dot(rows_now[...], wts[:, lanes], preferred_element_type=F32)
        up = jnp.dot(rows_now[...], wts[:, up_lanes], preferred_element_type=F32)
        incoming = hid[:, lanes].astype(F32)
        sig = 1.0 / (1.0 + jnp.exp(-gate))
        act = gate * sig
        slope = sig * (1.0 + gate * (1.0 - sig))
        grads[:, lanes] = (incoming * up * slope).astype(BF16)
        grads[:, up_lanes] = (incoming * act).astype(BF16)

    gate_step(0)
    gate_step(1)
    old_2 = gather_hop(rows_old, old_place, old_ss, old_rs, 2, old_1)
    share(-2)
    share(2)
    gate_step(2)

    def lanes_of(c):
        return slice(c * CHUNK, (c + 1) * CHUNK)

    moving = {}

    def push(c, way, hop):
        by = 1 - 2 * way
        lanes = lanes_of(c)
        value = term[now_place(chip((4 - hop) * by)), lanes]
        if (c, way, hop - 1) in moving:
            moving[c, way, hop - 1].wait_recv()
            value = value + (land_r, land_l)[way][hop - 1, :, lanes].astype(F32)
        src = (send_r, send_l)[way].at[hop, :, lanes]
        src[...] = value.astype(BF16)
        at = (way * 4 + hop) * CHUNKS + c
        moving[c, way, hop] = send(
            src,
            (land_r, land_l)[way].at[hop, :, lanes],
            red_ss.at[at],
            red_rs.at[at],
            device(-1 if hop == 3 else 0, by, 0),
        )

    order = (0, 2, 1, 3)
    own = {}

    def start_chunk(c):
        lanes = lanes_of(c)
        term[:, lanes] = lax.dot_general(
            grads[...], wts[lanes, :], (((1,), (1,)), ((), ())), preferred_element_type=F32
        )
        long = 0 if c < CHUNKS // 2 else 1
        push(c, long, 0)
        push(c, 1 - long, 1)
        send_o[:, lanes] = term[mine, lanes].astype(BF16)
        own[c] = send(
            send_o.at[:, lanes], land_o.at[:, lanes], own_ss.at[c], own_rs.at[c], device(-1, 0, 0)
        )

    start_chunk(order[0])
    start_chunk(order[1])
    old_3 = gather_hop(rows_old, old_place, old_ss, old_rs, 3, old_2)
    for way in range(2):
        for piece in range(PIECES):
            if (way, piece) not in old_3:
                old_2[way, piece].wait_recv()
    share(-3)
    share(3)
    start_chunk(order[2])
    start_chunk(order[3])

    def dw_step(i):
        rows = slice(i * 256, (i + 1) * 256)
        value = lax.dot_general(
            rows_old[:, rows], old[...], (((0,), (0,)), ((), ())), preferred_element_type=F32
        ).astype(BF16)
        dw_gate[rows, :] = value[:, 0:WIDTH]
        dw_up[rows, :] = value[:, WIDTH:BOTH]

    for turn in (1, 2, 3):
        for i, c in enumerate(order):
            long = 0 if c < CHUNKS // 2 else 1
            push(c, long, turn)
            if turn < 3:
                push(c, 1 - long, turn + 1)
            if turn == 1 and i == 0:
                for copy in old_3.values():
                    copy.wait_recv()
                share(4, 0, PIECE)
                share(4, PIECE, D)
                for copy in siblings:
                    copy.wait_recv()
            dw_step((turn - 1) * 4 + i)

    table_sent.wait_recv()
    back = tab_in[:, 0:TOK].astype(BF16)
    scale = tab_in[:, TOK : TOK + 1]
    last = s == sections - 1
    for c in order:
        lanes = lanes_of(c)
        own[c].wait_recv()
        moving[c, 0, 3].wait_recv()
        moving[c, 1, 3].wait_recv()
        total = (
            land_o[:, lanes].astype(F32)
            + land_r[3, :, lanes].astype(F32)
            + land_l[3, :, lanes].astype(F32)
        )
        spread = lax.dot_general(
            back, (scale * total).astype(BF16), (((0,), (0,)), ((), ())), preferred_element_type=F32
        )
        out[:, lanes] = jnp.where(last, 0.0, spread).astype(BF16)
    for copy in sent:
        copy.wait_send()


def shards(
    x_now, ids_now, gates_now, hidden_now, x_old, ids_old, gate_grad_old, up_grad_old, w_gate, w_up
):
    anywhere = pl.BlockSpec(memory_space=pl.ANY)
    dma = pltpu.SemaphoreType.DMA
    out, dw_gate, dw_up = pl.pallas_call(
        kernel,
        out_shape=(
            pltpu.VMEM((TOK, D), BF16),
            pltpu.VMEM((D, WIDTH), BF16),
            pltpu.VMEM((D, WIDTH), BF16),
        ),
        in_specs=[anywhere] * 10,
        out_specs=[pl.BlockSpec(memory_space=pltpu.VMEM)] * 3,
        scratch_shapes=[
            pltpu.VMEM((4, TOK), jnp.int32),
            pltpu.VMEM((4, TOK), F32),
            pltpu.VMEM((4, TOK), jnp.int32),
            pltpu.VMEM((TOK, D), BF16),
            pltpu.VMEM((TOK, D), BF16),
            pltpu.VMEM((LANE, BOTH), BF16),
            pltpu.VMEM((2 * LANE, BOTH), BF16),
            pltpu.VMEM((D, 2 * BOTH), BF16),
            pltpu.VMEM((LANE, D), BF16),
            pltpu.VMEM((2 * LANE, D), BF16),
            pltpu.VMEM((LANE, 2 * BOTH), BF16),
            pltpu.VMEM((LANE, D), F32),
            pltpu.VMEM((4, CAP, D), BF16),
            pltpu.VMEM((4, CAP, D), BF16),
            pltpu.VMEM((CAP, D), BF16),
            pltpu.VMEM((4, CAP, D), BF16),
            pltpu.VMEM((4, CAP, D), BF16),
            pltpu.VMEM((CAP, D), BF16),
            pltpu.VMEM((CAP, 2 * TOK), F32),
            pltpu.VMEM((CAP, 2 * TOK), F32),
            dma((11,)),
            dma((8 * PIECES,)),
            dma((8 * PIECES,)),
            dma((8 * PIECES,)),
            dma((8 * PIECES,)),
            dma((9,)),
            dma((9,)),
            dma((14,)),
            dma((14,)),
            dma((2,)),
            dma((2,)),
            dma((1,)),
            dma((1,)),
            dma((8 * CHUNKS,)),
            dma((8 * CHUNKS,)),
            dma((CHUNKS,)),
            dma((CHUNKS,)),
        ],
        compiler_params=pltpu.CompilerParams(
            collective_id=0, has_side_effects=True, vmem_limit_bytes=48 << 20
        ),
        cost_estimate=pl.CostEstimate(
            flops=3 * 2 * 512 * D * BOTH, bytes_accessed=16 << 20, transcendentals=512 * WIDTH
        ),
    )(
        ids_now[0].T, gates_now[0].T, ids_old[0].T, x_now[0], hidden_now[0], x_old[0],
        gate_grad_old[0], up_grad_old[0], w_gate[0], w_up[0],
    )
    return out[None], dw_gate[None], dw_up[None]


def solution(mesh):
    in_specs = (
        P("section", ("expert", "dp"), None),
        P("section", ("expert", "dp"), None),
        P("section", ("expert", "dp"), None),
        P("section", ("expert", "dp"), None),
        P("section", ("expert", "dp"), None),
        P("section", ("expert", "dp"), None),
        P("section", None, ("expert", "dp")),
        P("section", None, ("expert", "dp")),
        P("section", None, ("expert", "dp")),
        P("section", None, ("expert", "dp")),
    )
    out_specs = (
        P("section", ("expert", "dp"), None),
        P("section", None, ("expert", "dp")),
        P("section", None, ("expert", "dp")),
    )
    return jax.shard_map(shards, mesh=mesh, in_specs=in_specs, out_specs=out_specs, check_vma=False)
```

```python
import jax
import jax.numpy as jnp
from jax import lax
from jax.experimental import pallas as pl
from jax.experimental.pallas import tpu as pltpu
from jax.sharding import PartitionSpec as P

EXPERTS = 16
RING = 8
CAP = 32
TOK = 128
D = 3072
WIDTH = 384
BOTH = 2 * WIDTH
LANE = RING * CAP
PIECES = 2
PIECE = D // PIECES
CHUNKS = 4
CHUNK = D // CHUNKS
ORDER = (0, -1, 1, -2, 2, -3, 3, 4)
NEAR, FAR = slice(0, 5 * CAP), slice(5 * CAP, LANE)
MESH = pl.DeviceIdType.MESH
F32 = jnp.float32
BF16 = jnp.bfloat16


def routing(ids, expert):
    hits = (ids == expert).astype(F32)
    routed = jnp.sum(hits, axis=0, keepdims=True)
    earlier = lax.broadcasted_iota(jnp.int32, (TOK, TOK), 0) < lax.broadcasted_iota(
        jnp.int32, (TOK, TOK), 1
    )
    counts = jnp.dot(
        jnp.broadcast_to(routed, (16, TOK)).astype(BF16),
        earlier.astype(F32).astype(BF16),
        preferred_element_type=F32,
    )
    slot = counts[0:1].astype(jnp.int32)
    places = lax.broadcasted_iota(jnp.int32, (CAP, TOK), 0)
    table = jnp.where((slot == places) & (routed == 1.0), 1.0, 0.0)
    return table, hits


def kernel(
    ids_now, gates_now, ids_old, x_now, hidden, x_old, gate_old, up_old, w_gate, w_up,
    packed_grad, tab_in, dw_gate, dw_up,
    ids_now_v, gates_now_v, ids_old_v, x_now_v, x_old_v, hid, old, wts, rows_now, rows_old,
    grads, term, send_r, send_l, send_o, land_r, land_l, land_o, tab_out,
    load_sem, now_ss, now_rs, old_ss, old_rs, sib_ss, sib_rs, hid_ss, hid_rs, w_ss, w_rs,
    tab_ss, tab_rs, red_ss, red_rs, own_ss, own_rs,
):
    sections = lax.axis_size("section")
    s = lax.axis_index("section")
    e = lax.axis_index("expert")
    z = lax.axis_index("dp") * 2 + e // 2
    k = lax.rem(e, 2)
    expert = lax.rem(s, EXPERTS)

    def chip(by):
        return lax.rem(z + (by + RING), RING)

    def device(by_section, by_z, by_core):
        there = chip(by_z)
        return (
            lax.rem(s + (by_section + sections), sections),
            lax.rem(there, 2) * 2 + lax.rem(k + by_core, 2),
            there // 2,
        )

    def group(there, core):
        return (lax.rem(there, 2) * 2 + core) * 4 + there // 2

    sent = []

    def send(src, dst, ss, rs, to):
        copy = pltpu.make_async_remote_copy(
            src_ref=src, dst_ref=dst, send_sem=ss, recv_sem=rs, device_id=to, device_id_type=MESH
        )
        copy.start()
        sent.append(copy)
        return copy

    barrier = pltpu.get_barrier_semaphore()
    partners = [device(0, 1, 0), device(0, -1, 0), device(0, 0, 1)]
    partners += [device(-1, 0, 0), device(1, 0, 0)]
    for partner in partners:
        pl.semaphore_signal(barrier, inc=1, device_id=partner, device_id_type=MESH)

    loads = 0

    def load(src, dst):
        nonlocal loads
        copy = pltpu.make_async_copy(src, dst, load_sem.at[loads])
        copy.start()
        loads += 1
        return copy

    def columns(start, size, step=128):
        return pl.ds(pl.multiple_of(start, step), size)

    def place(by):
        at = ORDER.index((by + 3) % RING - 3) * CAP
        return slice(at, at + CAP)

    get_now = [load(ids_now, ids_now_v), load(gates_now, gates_now_v), load(x_now, x_now_v)]
    for copy in get_now:
        copy.wait()
    get_old = [load(ids_old, ids_old_v), load(x_old, x_old_v)]
    gate_place, up_place = columns(k * WIDTH, WIDTH), columns(BOTH + k * WIDTH, WIDTH)
    get_weights = [load(w_gate, wts.at[:, gate_place]), load(w_up, wts.at[:, up_place])]
    get_hidden = [
        load(
            hidden.at[:, columns(group(z, core) * WIDTH, WIDTH)],
            hid.at[place(0), core * WIDTH : (core + 1) * WIDTH],
        )
        for core in range(2)
    ]
    get_stored = [load(gate_old, old.at[:, 0:WIDTH]), load(up_old, old.at[:, WIDTH:BOTH])]

    table, hits = routing(ids_now_v[...], expert)
    rows_now[place(0), :] = jnp.dot(
        table.astype(BF16), x_now_v[...], preferred_element_type=F32
    ).astype(BF16)
    weight = jnp.sum(gates_now_v[...] * hits, axis=0, keepdims=True)
    coef = jnp.sum(table * weight, axis=1, keepdims=True)
    tab_out[:, 0:TOK] = table
    tab_out[:, TOK : 2 * TOK] = jnp.broadcast_to(coef, (CAP, TOK))

    pl.semaphore_wait(barrier, len(partners))

    def gather_hop(buf, src, dst, ss, rs, hop, waits):
        copies = {}
        for piece in range(PIECES):
            for way, by in enumerate((1, -1)):
                if hop == 3 and (piece < PIECES // 2) != (way == 0):
                    continue
                if waits is not None:
                    waits[way, piece].wait_recv()
                lanes = slice(piece * PIECE, (piece + 1) * PIECE)
                at = (way * 4 + hop) * PIECES + piece
                copies[way, piece] = send(
                    buf.at[src(hop, by), lanes],
                    buf.at[dst(hop, by), lanes],
                    ss.at[at],
                    rs.at[at],
                    device(0, by, 0),
                )
        return copies

    def now_hop(hop, waits):
        def src(hop, by):
            return place(-hop * by)

        def dst(hop, by):
            return place(-(hop + 1) * by)

        return gather_hop(rows_now, src, dst, now_ss, now_rs, hop, waits)

    def old_place(there):
        return pl.ds(pl.multiple_of(group(there, k) * CAP, CAP), CAP)

    def old_hop(hop, waits):
        def both(hop, by):
            return old_place(chip(-hop * by))

        return gather_hop(rows_old, both, both, old_ss, old_rs, hop, waits)

    def arrive(before, after):
        for key, copy in before.items():
            if key not in after:
                copy.wait_recv()

    siblings = []

    def share(by, first=0, last=D):
        block = rows_old.at[old_place(chip(by)), first:last]
        at = len(siblings)
        siblings.append(send(block, block, sib_ss.at[at], sib_rs.at[at], device(0, 0, 1)))

    hidden_sent = {}

    def send_hidden(by):
        there = chip(by)
        for core in range(2):
            at = (by % RING - 1) * 2 + core
            hidden_sent[by, core] = send(
                hidden.at[:, columns(group(there, core) * WIDTH, WIDTH)],
                hid.at[place(-by), core * WIDTH : (core + 1) * WIDTH],
                hid_ss.at[at],
                hid_rs.at[at],
                device(0, by, 0),
            )

    now_0 = now_hop(0, None)
    weights_sent = [
        send(w_gate, wts.at[:, gate_place], w_ss.at[0], w_rs.at[0], device(0, 0, 1)),
        send(w_up, wts.at[:, up_place], w_ss.at[1], w_rs.at[1], device(0, 0, 1)),
    ]
    for by in (1, -1):
        send_hidden(by)
    table_sent = send(tab_out, tab_in, tab_ss.at[0], tab_rs.at[0], device(-1, 0, 0))

    for copy in get_old:
        copy.wait()
    old_table, _ = routing(ids_old_v[...], expert)
    rows_old[old_place(z), :] = jnp.dot(
        old_table.astype(BF16), x_old_v[...], preferred_element_type=F32
    ).astype(BF16)

    old_0 = old_hop(0, None)
    share(0)
    now_1 = now_hop(1, now_0)
    for by in (2, -2):
        send_hidden(by)
    now_2 = now_hop(2, now_1)
    for by in (3, -3):
        send_hidden(by)

    for copy in get_weights + get_hidden + get_stored:
        copy.wait()
    for copy in weights_sent:
        copy.wait_recv()

    def gate_step(rows, j):
        lanes = slice(j * 256, (j + 1) * 256)
        up_lanes = slice(BOTH + j * 256, BOTH + (j + 1) * 256)
        gate = jnp.dot(rows_now[rows, :], wts[:, lanes], preferred_element_type=F32)
        up = jnp.dot(rows_now[rows, :], wts[:, up_lanes], preferred_element_type=F32)
        incoming = hid[rows, lanes].astype(F32)
        sig = 1.0 / (1.0 + jnp.exp(-gate))
        act = gate * sig
        slope = sig * (1.0 + gate * (1.0 - sig))
        grads[rows, lanes] = (incoming * up * slope).astype(BF16)
        grads[rows, up_lanes] = (incoming * act).astype(BF16)

    def lanes_of(c):
        return slice(c * CHUNK, (c + 1) * CHUNK)

    def term_step(rows, c):
        term[rows, lanes_of(c)] = lax.dot_general(
            grads[rows, :], wts[lanes_of(c), :], (((1,), (1,)), ((), ())), preferred_element_type=F32
        )

    for by in (1, -1, 2, -2):
        for core in range(2):
            hidden_sent[by, core].wait_recv()
    for j in range(3):
        gate_step(NEAR, j)
    now_3 = now_hop(3, now_2)
    send_hidden(4)
    for c in range(CHUNKS):
        term_step(NEAR, c)
    old_1 = old_hop(1, old_0)
    share(-1)
    share(1)

    moving = {}

    def push(c, way, hop):
        by = 1 - 2 * way
        lanes = lanes_of(c)
        value = term[place((4 - hop) * by), lanes]
        if (c, way, hop - 1) in moving:
            moving[c, way, hop - 1].wait_recv()
            value = value + (land_r, land_l)[way][hop - 1, :, lanes].astype(F32)
        src = (send_r, send_l)[way].at[hop, :, lanes]
        src[...] = value.astype(BF16)
        at = (way * 4 + hop) * CHUNKS + c
        moving[c, way, hop] = send(
            src,
            (land_r, land_l)[way].at[hop, :, lanes],
            red_ss.at[at],
            red_rs.at[at],
            device(-1 if hop == 3 else 0, by, 0),
        )

    order = (0, 2, 1, 3)

    def long_way(c):
        return 0 if c < CHUNKS // 2 else 1

    arrive(now_2, now_3)
    for copy in now_3.values():
        copy.wait_recv()
    for by in (3, -3, 4):
        for core in range(2):
            hidden_sent[by, core].wait_recv()
    for j in range(3):
        gate_step(FAR, j)
    for c in order:
        term_step(FAR, c)
        push(c, long_way(c), 0)
        push(c, 1 - long_way(c), 1)
    old_2 = old_hop(2, old_1)
    share(-2)
    share(2)
    send_o[...] = term[place(0), :].astype(BF16)
    own = send(send_o, land_o, own_ss.at[0], own_rs.at[0], device(-1, 0, 0))

    def dw_step(i):
        rows = slice(i * 256, (i + 1) * 256)
        value = lax.dot_general(
            rows_old[:, rows], old[...], (((0,), (0,)), ((), ())), preferred_element_type=F32
        ).astype(BF16)
        dw_gate[rows, :] = value[:, 0:WIDTH]
        dw_up[rows, :] = value[:, WIDTH:BOTH]

    for c in order:
        push(c, long_way(c), 1)
    for c in order:
        push(c, 1 - long_way(c), 2)
    old_3 = old_hop(3, old_2)
    arrive(old_2, old_3)
    share(-3)
    share(3)
    for c in order:
        push(c, long_way(c), 2)
    for c in order:
        push(c, 1 - long_way(c), 3)
    for copy in old_3.values():
        copy.wait_recv()
    share(4, 0, D // 2)
    share(4, D // 2, D)
    for c in order:
        push(c, long_way(c), 3)
    for copy in siblings:
        copy.wait_recv()
    for i in range(12):
        dw_step(i)

    table_sent.wait_recv()
    own.wait_recv()
    scale = tab_in[:, TOK : TOK + 1]
    for c in order:
        lanes = lanes_of(c)
        moving[c, 0, 3].wait_recv()
        moving[c, 1, 3].wait_recv()
        total = (
            land_o[:, lanes].astype(F32)
            + land_r[3, :, lanes].astype(F32)
            + land_l[3, :, lanes].astype(F32)
        )
        packed_grad[:, lanes] = (scale * total).astype(BF16)
    for copy in sent:
        copy.wait_send()


def finish(packed_grad, tab, dw_gate, dw_up, out, out_gate, out_up, spread, sem):
    copies = []
    for src, dst in ((dw_gate, out_gate), (dw_up, out_up)):
        for part in range(2):
            rows = slice(part * (D // 2), (part + 1) * (D // 2))
            copies.append(pltpu.make_async_copy(src.at[rows], dst.at[rows], sem.at[len(copies)]))
            copies[-1].start()
    last = lax.axis_index("section") == lax.axis_size("section") - 1
    back = tab[:, 0:TOK].astype(BF16)
    for c in range(2):
        lanes = slice(c * (D // 2), (c + 1) * (D // 2))
        value = lax.dot_general(
            back, packed_grad[:, lanes], (((0,), (0,)), ((), ())), preferred_element_type=F32
        )
        spread[:, lanes] = jnp.where(last, 0.0, value).astype(BF16)
        copies.append(pltpu.make_async_copy(spread.at[:, lanes], out.at[:, lanes], sem.at[4 + c]))
        copies[-1].start()
    for copy in copies:
        copy.wait()


def shards(
    x_now, ids_now, gates_now, hidden_now, x_old, ids_old, gate_grad_old, up_grad_old, w_gate, w_up
):
    anywhere = pl.BlockSpec(memory_space=pl.ANY)
    dma = pltpu.SemaphoreType.DMA
    inputs = [
        ids_now[0].T, gates_now[0].T, ids_old[0].T, x_now[0], hidden_now[0], x_old[0],
        gate_grad_old[0], up_grad_old[0], w_gate[0], w_up[0],
    ]
    inputs = [pltpu.with_memory_space_constraint(array, pltpu.HBM) for array in inputs]
    packed_grad, tab, dw_gate, dw_up = pl.pallas_call(
        kernel,
        out_shape=(
            pltpu.VMEM((CAP, D), BF16),
            pltpu.VMEM((CAP, 2 * TOK), F32),
            pltpu.VMEM((D, WIDTH), BF16),
            pltpu.VMEM((D, WIDTH), BF16),
        ),
        in_specs=[anywhere] * 10,
        out_specs=[pl.BlockSpec(memory_space=pltpu.VMEM)] * 4,
        scratch_shapes=[
            pltpu.VMEM((4, TOK), jnp.int32),
            pltpu.VMEM((4, TOK), F32),
            pltpu.VMEM((4, TOK), jnp.int32),
            pltpu.VMEM((TOK, D), BF16),
            pltpu.VMEM((TOK, D), BF16),
            pltpu.VMEM((LANE, BOTH), BF16),
            pltpu.VMEM((2 * LANE, BOTH), BF16),
            pltpu.VMEM((D, 2 * BOTH), BF16),
            pltpu.VMEM((LANE, D), BF16),
            pltpu.VMEM((2 * LANE, D), BF16),
            pltpu.VMEM((LANE, 2 * BOTH), BF16),
            pltpu.VMEM((LANE, D), F32),
            pltpu.VMEM((4, CAP, D), BF16),
            pltpu.VMEM((4, CAP, D), BF16),
            pltpu.VMEM((CAP, D), BF16),
            pltpu.VMEM((4, CAP, D), BF16),
            pltpu.VMEM((4, CAP, D), BF16),
            pltpu.VMEM((CAP, D), BF16),
            pltpu.VMEM((CAP, 2 * TOK), F32),
            dma((11,)),
            dma((8 * PIECES,)),
            dma((8 * PIECES,)),
            dma((8 * PIECES,)),
            dma((8 * PIECES,)),
            dma((9,)),
            dma((9,)),
            dma((14,)),
            dma((14,)),
            dma((2,)),
            dma((2,)),
            dma((1,)),
            dma((1,)),
            dma((8 * CHUNKS,)),
            dma((8 * CHUNKS,)),
            dma((1,)),
            dma((1,)),
        ],
        compiler_params=pltpu.CompilerParams(
            collective_id=0, has_side_effects=True, vmem_limit_bytes=48 << 20
        ),
        cost_estimate=pl.CostEstimate(
            flops=3 * 2 * 512 * D * BOTH, bytes_accessed=16 << 20, transcendentals=512 * WIDTH
        ),
    )(*inputs)
    out, dw_gate, dw_up = pl.pallas_call(
        finish,
        out_shape=(
            jax.ShapeDtypeStruct((TOK, D), BF16),
            jax.ShapeDtypeStruct((D, WIDTH), BF16),
            jax.ShapeDtypeStruct((D, WIDTH), BF16),
        ),
        in_specs=[pl.BlockSpec(memory_space=pltpu.VMEM)] * 4,
        out_specs=[pl.BlockSpec(memory_space=pltpu.HBM)] * 3,
        scratch_shapes=[pltpu.VMEM((TOK, D), BF16), dma((6,))],
        compiler_params=pltpu.CompilerParams(vmem_limit_bytes=16 << 20),
    )(packed_grad, tab, dw_gate, dw_up)
    return out[None], dw_gate[None], dw_up[None]


def solution(mesh):
    in_specs = (
        P("section", ("expert", "dp"), None),
        P("section", ("expert", "dp"), None),
        P("section", ("expert", "dp"), None),
        P("section", ("expert", "dp"), None),
        P("section", ("expert", "dp"), None),
        P("section", ("expert", "dp"), None),
        P("section", None, ("expert", "dp")),
        P("section", None, ("expert", "dp")),
        P("section", None, ("expert", "dp")),
        P("section", None, ("expert", "dp")),
    )
    out_specs = (
        P("section", ("expert", "dp"), None),
        P("section", None, ("expert", "dp")),
        P("section", None, ("expert", "dp")),
    )
    return jax.shard_map(shards, mesh=mesh, in_specs=in_specs, out_specs=out_specs, check_vma=False)
```

```python
import jax
import jax.numpy as jnp
from jax import lax
from jax.experimental import pallas as pl
from jax.experimental.pallas import tpu as pltpu
from jax.sharding import PartitionSpec as P

EXPERTS = 16
RING = 8
CAP = 32
TOK = 128
D = 3072
WIDTH = 384
BOTH = 2 * WIDTH
LANE = RING * CAP
PIECES = 2
PIECE = D // PIECES
CHUNKS = 4
CHUNK = D // CHUNKS
ORDER = (0, -1, 1, -2, 2, -3, 3, 4)
NEAR, FAR = slice(0, 5 * CAP), slice(5 * CAP, LANE)
MESH = pl.DeviceIdType.MESH
F32 = jnp.float32
BF16 = jnp.bfloat16


def routing(ids, expert):
    hits = (ids == expert).astype(F32)
    routed = jnp.sum(hits, axis=0, keepdims=True)
    earlier = lax.broadcasted_iota(jnp.int32, (TOK, TOK), 0) < lax.broadcasted_iota(
        jnp.int32, (TOK, TOK), 1
    )
    counts = jnp.dot(
        jnp.broadcast_to(routed, (16, TOK)).astype(BF16),
        earlier.astype(F32).astype(BF16),
        preferred_element_type=F32,
    )
    slot = counts[0:1].astype(jnp.int32)
    places = lax.broadcasted_iota(jnp.int32, (CAP, TOK), 0)
    table = jnp.where((slot == places) & (routed == 1.0), 1.0, 0.0)
    return table, hits


def kernel(
    ids_now, gates_now, ids_old, x_now, hidden, x_old, gate_old, up_old, w_gate, w_up,
    packed_grad, tab_in, dw_gate, dw_up,
    ids_now_v, gates_now_v, ids_old_v, x_now_v, x_old_v, hid, old, wts, rows_now, rows_old,
    grads, term, send_r, send_l, send_o, land_r, land_l, land_o, tab_out,
    load_sem, now_ss, now_rs, old_ss, old_rs, sib_ss, sib_rs, hid_ss, hid_rs, w_ss, w_rs,
    tab_ss, tab_rs, red_ss, red_rs, own_ss, own_rs,
):
    sections = lax.axis_size("section")
    s = lax.axis_index("section")
    e = lax.axis_index("expert")
    z = lax.axis_index("dp") * 2 + e // 2
    k = lax.rem(e, 2)
    expert = lax.rem(s, EXPERTS)

    def chip(by):
        return lax.rem(z + (by + RING), RING)

    def device(by_section, by_z, by_core):
        there = chip(by_z)
        return (
            lax.rem(s + (by_section + sections), sections),
            lax.rem(there, 2) * 2 + lax.rem(k + by_core, 2),
            there // 2,
        )

    def group(there, core):
        return (lax.rem(there, 2) * 2 + core) * 4 + there // 2

    sent = []

    def send(src, dst, ss, rs, to):
        copy = pltpu.make_async_remote_copy(
            src_ref=src, dst_ref=dst, send_sem=ss, recv_sem=rs, device_id=to, device_id_type=MESH
        )
        copy.start()
        sent.append(copy)
        return copy

    barrier = pltpu.get_barrier_semaphore()
    partners = [device(0, 1, 0), device(0, -1, 0), device(0, 0, 1), device(1, 0, 0)]
    for partner in partners:
        pl.semaphore_signal(barrier, inc=1, device_id=partner, device_id_type=MESH)

    loads = 0

    def load(src, dst):
        nonlocal loads
        copy = pltpu.make_async_copy(src, dst, load_sem.at[loads])
        copy.start()
        loads += 1
        return copy

    def columns(start, size, step=128):
        return pl.ds(pl.multiple_of(start, step), size)

    def place(by):
        at = ORDER.index((by + 3) % RING - 3) * CAP
        return slice(at, at + CAP)

    get_now = [load(ids_now, ids_now_v), load(gates_now, gates_now_v), load(x_now, x_now_v)]
    for copy in get_now:
        copy.wait()
    get_old = [load(ids_old, ids_old_v), load(x_old, x_old_v)]
    gate_place, up_place = columns(k * WIDTH, WIDTH), columns(BOTH + k * WIDTH, WIDTH)
    get_weights = [load(w_gate, wts.at[:, gate_place]), load(w_up, wts.at[:, up_place])]
    get_hidden = [
        load(
            hidden.at[:, columns(group(z, core) * WIDTH, WIDTH)],
            hid.at[place(0), core * WIDTH : (core + 1) * WIDTH],
        )
        for core in range(2)
    ]
    get_stored = [load(gate_old, old.at[:, 0:WIDTH]), load(up_old, old.at[:, WIDTH:BOTH])]

    table, hits = routing(ids_now_v[...], expert)
    rows_now[place(0), :] = jnp.dot(
        table.astype(BF16), x_now_v[...], preferred_element_type=F32
    ).astype(BF16)
    weight = jnp.sum(gates_now_v[...] * hits, axis=0, keepdims=True)
    coef = jnp.sum(table * weight, axis=1, keepdims=True)
    tab_out[:, 0:TOK] = table
    tab_out[:, TOK : 2 * TOK] = jnp.broadcast_to(coef, (CAP, TOK))

    pl.semaphore_wait(barrier, len(partners))

    def gather_hop(buf, src, dst, ss, rs, hop, waits, turns):
        copies = {}
        for turn in turns:
            if hop == 3 and turn >= PIECES // 2:
                continue
            for way, by in enumerate((1, -1)):
                if waits is not None:
                    waits[way, turn].wait_recv()
                piece = turn if way == 0 else PIECES - 1 - turn
                lanes = slice(piece * PIECE, (piece + 1) * PIECE)
                at = (way * 4 + hop) * PIECES + turn
                copies[way, turn] = send(
                    buf.at[src(hop, by), lanes],
                    buf.at[dst(hop, by), lanes],
                    ss.at[at],
                    rs.at[at],
                    device(0, by, 0),
                )
        return copies

    def now_hop(hop, waits, turns=range(PIECES)):
        def src(hop, by):
            return place(-hop * by)

        def dst(hop, by):
            return place(-(hop + 1) * by)

        return gather_hop(rows_now, src, dst, now_ss, now_rs, hop, waits, turns)

    def old_place(there):
        return pl.ds(pl.multiple_of(group(there, k) * CAP, CAP), CAP)

    def old_hop(hop, waits, turns=range(PIECES)):
        def both(hop, by):
            return old_place(chip(-hop * by))

        return gather_hop(rows_old, both, both, old_ss, old_rs, hop, waits, turns)

    def arrive(before, after):
        for key, copy in before.items():
            if key not in after:
                copy.wait_recv()

    siblings = []

    def share(by, first=0, last=D):
        block = rows_old.at[old_place(chip(by)), first:last]
        at = len(siblings)
        siblings.append(send(block, block, sib_ss.at[at], sib_rs.at[at], device(0, 0, 1)))

    hidden_sent = {}

    def send_hidden(by):
        there = chip(by)
        for core in range(2):
            at = (by % RING - 1) * 2 + core
            hidden_sent[by, core] = send(
                hidden.at[:, columns(group(there, core) * WIDTH, WIDTH)],
                hid.at[place(-by), core * WIDTH : (core + 1) * WIDTH],
                hid_ss.at[at],
                hid_rs.at[at],
                device(0, by, 0),
            )

    now_0 = now_hop(0, None)
    weights_sent = [
        send(w_gate, wts.at[:, gate_place], w_ss.at[0], w_rs.at[0], device(0, 0, 1)),
        send(w_up, wts.at[:, up_place], w_ss.at[1], w_rs.at[1], device(0, 0, 1)),
    ]
    for by in (1, -1):
        send_hidden(by)
    table_sent = send(tab_out, tab_in, tab_ss.at[0], tab_rs.at[0], device(-1, 0, 0))

    for copy in get_old:
        copy.wait()
    old_table, _ = routing(ids_old_v[...], expert)
    rows_old[old_place(z), :] = jnp.dot(
        old_table.astype(BF16), x_old_v[...], preferred_element_type=F32
    ).astype(BF16)

    share(0)
    now_1 = now_hop(1, now_0)
    for by in (2, -2):
        send_hidden(by)
    now_2 = now_hop(2, now_1)
    for by in (3, -3):
        send_hidden(by)

    for copy in get_weights + get_hidden + get_stored:
        copy.wait()
    for copy in weights_sent:
        copy.wait_recv()

    def gate_step(rows, j):
        lanes = slice(j * 256, (j + 1) * 256)
        up_lanes = slice(BOTH + j * 256, BOTH + (j + 1) * 256)
        gate = jnp.dot(rows_now[rows, :], wts[:, lanes], preferred_element_type=F32)
        up = jnp.dot(rows_now[rows, :], wts[:, up_lanes], preferred_element_type=F32)
        incoming = hid[rows, lanes].astype(F32)
        sig = 1.0 / (1.0 + jnp.exp(-gate))
        act = gate * sig
        slope = sig * (1.0 + gate * (1.0 - sig))
        grads[rows, lanes] = (incoming * up * slope).astype(BF16)
        grads[rows, up_lanes] = (incoming * act).astype(BF16)

    def lanes_of(c):
        return slice(c * CHUNK, (c + 1) * CHUNK)

    def term_step(rows, c):
        term[rows, lanes_of(c)] = lax.dot_general(
            grads[rows, :], wts[lanes_of(c), :], (((1,), (1,)), ((), ())), preferred_element_type=F32
        )

    for by in (1, -1, 2, -2):
        for core in range(2):
            hidden_sent[by, core].wait_recv()
    for j in range(3):
        gate_step(NEAR, j)
    for way in range(2):
        now_2[way, 0].wait_recv()
    send_hidden(4)
    now_3 = now_hop(3, None)
    old_0 = old_hop(0, None)
    for c in range(CHUNKS):
        term_step(NEAR, c)

    moving = {}

    def push(c, way, hop):
        by = 1 - 2 * way
        lanes = lanes_of(c)
        value = term[place((4 - hop) * by), lanes]
        if (c, way, hop - 1) in moving:
            moving[c, way, hop - 1].wait_recv()
            value = value + (land_r, land_l)[way][hop - 1, :, lanes].astype(F32)
        src = (send_r, send_l)[way].at[hop, :, lanes]
        src[...] = value.astype(BF16)
        at = (way * 4 + hop) * CHUNKS + c
        moving[c, way, hop] = send(
            src,
            (land_r, land_l)[way].at[hop, :, lanes],
            red_ss.at[at],
            red_rs.at[at],
            device(-1 if hop == 3 else 0, by, 0),
        )

    order = (0, 2, 1, 3)

    def long_way(c):
        return 0 if c < CHUNKS // 2 else 1

    def dw_step(i):
        rows = slice(i * 256, (i + 1) * 256)
        value = lax.dot_general(
            rows_old[:, rows], old[...], (((0,), (0,)), ((), ())), preferred_element_type=F32
        ).astype(BF16)
        dw_gate[rows, :] = value[:, 0:WIDTH]
        dw_up[rows, :] = value[:, WIDTH:BOTH]

    arrive(now_2, now_3)
    for copy in now_3.values():
        copy.wait_recv()
    for by in (3, -3, 4):
        for core in range(2):
            hidden_sent[by, core].wait_recv()
    for j in range(3):
        gate_step(FAR, j)
    old_1, old_2 = {}, {}
    for turn in range(PIECES):
        old_1 |= old_hop(1, old_0, [turn])
        for c in order[2 * turn : 2 * turn + 2]:
            term_step(FAR, c)
            push(c, long_way(c), 0)
            push(c, 1 - long_way(c), 1)
    share(-1)
    share(1)
    send_o[...] = term[place(0), :].astype(BF16)
    own = send(send_o, land_o, own_ss.at[0], own_rs.at[0], device(-1, 0, 0))
    for turn in range(PIECES):
        old_2 |= old_hop(2, old_1, [turn])
        for c in order[2 * turn : 2 * turn + 2]:
            push(c, long_way(c), 1)
            push(c, 1 - long_way(c), 2)
    share(-2)
    share(2)
    old_3 = old_hop(3, old_2)
    for c in order:
        push(c, long_way(c), 2)
    for c in order:
        push(c, 1 - long_way(c), 3)
    arrive(old_2, old_3)
    share(-3)
    share(3)
    for copy in old_3.values():
        copy.wait_recv()
    share(4, 0, D // 2)
    share(4, D // 2, D)
    for c in order:
        push(c, long_way(c), 3)
    for copy in siblings:
        copy.wait_recv()
    for i in range(12):
        dw_step(i)

    for copy in sent:
        copy.wait_send()
    table_sent.wait_recv()
    own.wait_recv()
    scale = tab_in[:, TOK : TOK + 1]
    for c in order:
        lanes = lanes_of(c)
        moving[c, 0, 3].wait_recv()
        moving[c, 1, 3].wait_recv()
        total = (
            land_o[:, lanes].astype(F32)
            + land_r[3, :, lanes].astype(F32)
            + land_l[3, :, lanes].astype(F32)
        )
        packed_grad[:, lanes] = (scale * total).astype(BF16)


def finish(packed_grad, tab, dw_gate, dw_up, out, out_gate, out_up, spread, sem):
    copies = []
    for src, dst in ((dw_gate, out_gate), (dw_up, out_up)):
        for part in range(2):
            rows = slice(part * (D // 2), (part + 1) * (D // 2))
            copies.append(pltpu.make_async_copy(src.at[rows], dst.at[rows], sem.at[len(copies)]))
            copies[-1].start()
    last = lax.axis_index("section") == lax.axis_size("section") - 1
    back = tab[:, 0:TOK].astype(BF16)
    for c in range(2):
        lanes = slice(c * (D // 2), (c + 1) * (D // 2))
        value = lax.dot_general(
            back, packed_grad[:, lanes], (((0,), (0,)), ((), ())), preferred_element_type=F32
        )
        spread[:, lanes] = jnp.where(last, 0.0, value).astype(BF16)
        copies.append(pltpu.make_async_copy(spread.at[:, lanes], out.at[:, lanes], sem.at[4 + c]))
        copies[-1].start()
    for copy in copies:
        copy.wait()


def shards(
    x_now, ids_now, gates_now, hidden_now, x_old, ids_old, gate_grad_old, up_grad_old, w_gate, w_up
):
    anywhere = pl.BlockSpec(memory_space=pl.ANY)
    dma = pltpu.SemaphoreType.DMA
    inputs = [
        ids_now[0].T, gates_now[0].T, ids_old[0].T, x_now[0], hidden_now[0], x_old[0],
        gate_grad_old[0], up_grad_old[0], w_gate[0], w_up[0],
    ]
    inputs = [pltpu.with_memory_space_constraint(array, pltpu.HBM) for array in inputs]
    packed_grad, tab, dw_gate, dw_up = pl.pallas_call(
        kernel,
        out_shape=(
            pltpu.VMEM((CAP, D), BF16),
            pltpu.VMEM((CAP, 2 * TOK), F32),
            pltpu.VMEM((D, WIDTH), BF16),
            pltpu.VMEM((D, WIDTH), BF16),
        ),
        in_specs=[anywhere] * 10,
        out_specs=[pl.BlockSpec(memory_space=pltpu.VMEM)] * 4,
        scratch_shapes=[
            pltpu.VMEM((4, TOK), jnp.int32),
            pltpu.VMEM((4, TOK), F32),
            pltpu.VMEM((4, TOK), jnp.int32),
            pltpu.VMEM((TOK, D), BF16),
            pltpu.VMEM((TOK, D), BF16),
            pltpu.VMEM((LANE, BOTH), BF16),
            pltpu.VMEM((2 * LANE, BOTH), BF16),
            pltpu.VMEM((D, 2 * BOTH), BF16),
            pltpu.VMEM((LANE, D), BF16),
            pltpu.VMEM((2 * LANE, D), BF16),
            pltpu.VMEM((LANE, 2 * BOTH), BF16),
            pltpu.VMEM((LANE, D), F32),
            pltpu.VMEM((4, CAP, D), BF16),
            pltpu.VMEM((4, CAP, D), BF16),
            pltpu.VMEM((CAP, D), BF16),
            pltpu.VMEM((4, CAP, D), BF16),
            pltpu.VMEM((4, CAP, D), BF16),
            pltpu.VMEM((CAP, D), BF16),
            pltpu.VMEM((CAP, 2 * TOK), F32),
            dma((11,)),
            dma((8 * PIECES,)),
            dma((8 * PIECES,)),
            dma((8 * PIECES,)),
            dma((8 * PIECES,)),
            dma((9,)),
            dma((9,)),
            dma((14,)),
            dma((14,)),
            dma((2,)),
            dma((2,)),
            dma((1,)),
            dma((1,)),
            dma((8 * CHUNKS,)),
            dma((8 * CHUNKS,)),
            dma((1,)),
            dma((1,)),
        ],
        compiler_params=pltpu.CompilerParams(
            collective_id=0, has_side_effects=True, vmem_limit_bytes=48 << 20
        ),
        cost_estimate=pl.CostEstimate(
            flops=3 * 2 * 512 * D * BOTH, bytes_accessed=16 << 20, transcendentals=512 * WIDTH
        ),
    )(*inputs)
    out, dw_gate, dw_up = pl.pallas_call(
        finish,
        out_shape=(
            jax.ShapeDtypeStruct((TOK, D), BF16),
            jax.ShapeDtypeStruct((D, WIDTH), BF16),
            jax.ShapeDtypeStruct((D, WIDTH), BF16),
        ),
        in_specs=[pl.BlockSpec(memory_space=pltpu.VMEM)] * 4,
        out_specs=[pl.BlockSpec(memory_space=pltpu.HBM)] * 3,
        scratch_shapes=[pltpu.VMEM((TOK, D), BF16), dma((6,))],
        compiler_params=pltpu.CompilerParams(vmem_limit_bytes=16 << 20),
    )(packed_grad, tab, dw_gate, dw_up)
    return out[None], dw_gate[None], dw_up[None]


def solution(mesh):
    in_specs = (
        P("section", ("expert", "dp"), None),
        P("section", ("expert", "dp"), None),
        P("section", ("expert", "dp"), None),
        P("section", ("expert", "dp"), None),
        P("section", ("expert", "dp"), None),
        P("section", ("expert", "dp"), None),
        P("section", None, ("expert", "dp")),
        P("section", None, ("expert", "dp")),
        P("section", None, ("expert", "dp")),
        P("section", None, ("expert", "dp")),
    )
    out_specs = (
        P("section", ("expert", "dp"), None),
        P("section", None, ("expert", "dp")),
        P("section", None, ("expert", "dp")),
    )
    return jax.shard_map(shards, mesh=mesh, in_specs=in_specs, out_specs=out_specs, check_vma=False)
```

```python
import jax
import jax.numpy as jnp
from jax import lax
from jax.experimental import pallas as pl
from jax.experimental.pallas import tpu as pltpu
from jax.sharding import PartitionSpec as P

EXPERTS = 16
RING = 8
CAP = 32
TOK = 128
D = 3072
WIDTH = 384
BOTH = 2 * WIDTH
LANE = RING * CAP
PIECES = 2
PIECE = D // PIECES
CHUNKS = 4
CHUNK = D // CHUNKS
ORDER = (0, -1, 1, -2, 2, -3, 3, 4)
NEAR, FAR = slice(0, 5 * CAP), slice(5 * CAP, LANE)
MESH = pl.DeviceIdType.MESH
F32 = jnp.float32
BF16 = jnp.bfloat16


def routing(ids, expert):
    hits = (ids == expert).astype(F32)
    routed = jnp.sum(hits, axis=0, keepdims=True)
    earlier = lax.broadcasted_iota(jnp.int32, (TOK, TOK), 0) < lax.broadcasted_iota(
        jnp.int32, (TOK, TOK), 1
    )
    counts = jnp.dot(
        jnp.broadcast_to(routed, (16, TOK)).astype(BF16),
        earlier.astype(F32).astype(BF16),
        preferred_element_type=F32,
    )
    slot = counts[0:1].astype(jnp.int32)
    places = lax.broadcasted_iota(jnp.int32, (CAP, TOK), 0)
    table = jnp.where((slot == places) & (routed == 1.0), 1.0, 0.0)
    return table, hits


def kernel(
    ids_now, gates_now, ids_old, x_now, hidden, x_old, gate_old, up_old, w_gate, w_up,
    packed_grad, tab_in, dw_gate, dw_up,
    ids_now_v, gates_now_v, ids_old_v, x_now_v, x_old_v, hid, old, wts, rows_now, rows_old,
    grads, term, send_r, send_l, send_o, land_r, land_l, land_o, tab_out,
    load_sem, now_ss, now_rs, old_ss, old_rs, sib_ss, sib_rs, hid_ss, hid_rs, w_ss, w_rs,
    tab_ss, tab_rs, red_ss, red_rs, own_ss, own_rs,
):
    sections = lax.axis_size("section")
    s = lax.axis_index("section")
    e = lax.axis_index("expert")
    z = lax.axis_index("dp") * 2 + e // 2
    k = lax.rem(e, 2)
    expert = lax.rem(s, EXPERTS)

    def chip(by):
        return lax.rem(z + (by + RING), RING)

    def device(by_section, by_z, by_core):
        there = chip(by_z)
        return (
            lax.rem(s + (by_section + sections), sections),
            lax.rem(there, 2) * 2 + lax.rem(k + by_core, 2),
            there // 2,
        )

    def group(there, core):
        return (lax.rem(there, 2) * 2 + core) * 4 + there // 2

    sent = []

    def send(src, dst, ss, rs, to):
        copy = pltpu.make_async_remote_copy(
            src_ref=src, dst_ref=dst, send_sem=ss, recv_sem=rs, device_id=to, device_id_type=MESH
        )
        copy.start()
        sent.append(copy)
        return copy

    barrier = pltpu.get_barrier_semaphore()
    partners = [device(0, 1, 0), device(0, -1, 0), device(0, 0, 1), device(1, 0, 0)]
    for partner in partners:
        pl.semaphore_signal(barrier, inc=1, device_id=partner, device_id_type=MESH)

    loads = 0

    def load(src, dst):
        nonlocal loads
        copy = pltpu.make_async_copy(src, dst, load_sem.at[loads])
        copy.start()
        loads += 1
        return copy

    def columns(start, size, step=128):
        return pl.ds(pl.multiple_of(start, step), size)

    def place(by):
        at = ORDER.index((by + 3) % RING - 3) * CAP
        return slice(at, at + CAP)

    get_now = [load(ids_now, ids_now_v), load(gates_now, gates_now_v), load(x_now, x_now_v)]
    gate_place, up_place = columns(k * WIDTH, WIDTH), columns(BOTH + k * WIDTH, WIDTH)
    hidden_sent = {}

    def send_hidden(by):
        there = chip(by)
        for core in range(2):
            at = (by % RING - 1) * 2 + core
            hidden_sent[by, core] = send(
                hidden.at[:, columns(group(there, core) * WIDTH, WIDTH)],
                hid.at[place(-by), core * WIDTH : (core + 1) * WIDTH],
                hid_ss.at[at],
                hid_rs.at[at],
                device(0, by, 0),
            )

    pl.semaphore_wait(barrier, len(partners))
    for by in (1, -1):
        send_hidden(by)
    for copy in get_now:
        copy.wait()
    table, hits = routing(ids_now_v[...], expert)
    rows_now[place(0), :] = jnp.dot(
        table.astype(BF16), x_now_v[...], preferred_element_type=F32
    ).astype(BF16)

    def gather_hop(buf, src, dst, ss, rs, hop, waits, turns):
        copies = {}
        for turn in turns:
            if hop == 3 and turn >= PIECES // 2:
                continue
            for way, by in enumerate((1, -1)):
                if waits is not None:
                    waits[way, turn].wait_recv()
                piece = turn if way == 0 else PIECES - 1 - turn
                lanes = slice(piece * PIECE, (piece + 1) * PIECE)
                at = (way * 4 + hop) * PIECES + turn
                copies[way, turn] = send(
                    buf.at[src(hop, by), lanes],
                    buf.at[dst(hop, by), lanes],
                    ss.at[at],
                    rs.at[at],
                    device(0, by, 0),
                )
        return copies

    def now_hop(hop, waits, turns=range(PIECES)):
        def src(hop, by):
            return place(-hop * by)

        def dst(hop, by):
            return place(-(hop + 1) * by)

        return gather_hop(rows_now, src, dst, now_ss, now_rs, hop, waits, turns)

    def old_place(there):
        return pl.ds(pl.multiple_of(group(there, k) * CAP, CAP), CAP)

    def old_hop(hop, waits, turns=range(PIECES)):
        def both(hop, by):
            return old_place(chip(-hop * by))

        return gather_hop(rows_old, both, both, old_ss, old_rs, hop, waits, turns)

    def arrive(before, after):
        for key, copy in before.items():
            if key not in after:
                copy.wait_recv()

    siblings = []

    def share(by, first=0, last=D):
        block = rows_old.at[old_place(chip(by)), first:last]
        at = len(siblings)
        siblings.append(send(block, block, sib_ss.at[at], sib_rs.at[at], device(0, 0, 1)))

    now_0 = now_hop(0, None)
    get_old = [load(ids_old, ids_old_v), load(x_old, x_old_v)]
    get_weights = [load(w_gate, wts.at[:, gate_place]), load(w_up, wts.at[:, up_place])]
    get_hidden = [
        load(
            hidden.at[:, columns(group(z, core) * WIDTH, WIDTH)],
            hid.at[place(0), core * WIDTH : (core + 1) * WIDTH],
        )
        for core in range(2)
    ]
    get_stored = [load(gate_old, old.at[:, 0:WIDTH]), load(up_old, old.at[:, WIDTH:BOTH])]

    weights_sent = [
        send(w_gate, wts.at[:, gate_place], w_ss.at[0], w_rs.at[0], device(0, 0, 1)),
        send(w_up, wts.at[:, up_place], w_ss.at[1], w_rs.at[1], device(0, 0, 1)),
    ]
    weight = jnp.sum(gates_now_v[...] * hits, axis=0, keepdims=True)
    coef = jnp.sum(table * weight, axis=1, keepdims=True)
    tab_out[:, 0:TOK] = table
    tab_out[:, TOK : 2 * TOK] = jnp.broadcast_to(coef, (CAP, TOK))

    table_sent = send(tab_out, tab_in, tab_ss.at[0], tab_rs.at[0], device(-1, 0, 0))

    for copy in get_old:
        copy.wait()
    old_table, _ = routing(ids_old_v[...], expert)
    rows_old[old_place(z), :] = jnp.dot(
        old_table.astype(BF16), x_old_v[...], preferred_element_type=F32
    ).astype(BF16)

    share(0)
    now_1 = now_hop(1, now_0)
    for by in (2, -2):
        send_hidden(by)
    now_2 = now_hop(2, now_1)
    for by in (3, -3):
        send_hidden(by)

    for copy in get_weights + get_hidden + get_stored:
        copy.wait()
    for copy in weights_sent:
        copy.wait_recv()

    def gate_step(rows, j):
        lanes = slice(j * 256, (j + 1) * 256)
        up_lanes = slice(BOTH + j * 256, BOTH + (j + 1) * 256)
        gate = jnp.dot(rows_now[rows, :], wts[:, lanes], preferred_element_type=F32)
        up = jnp.dot(rows_now[rows, :], wts[:, up_lanes], preferred_element_type=F32)
        incoming = hid[rows, lanes].astype(F32)
        sig = jax.nn.sigmoid(gate)
        act = gate * sig
        slope = sig * (1.0 + gate * (1.0 - sig))
        grads[rows, lanes] = (incoming * up * slope).astype(BF16)
        grads[rows, up_lanes] = (incoming * act).astype(BF16)

    def lanes_of(c):
        return slice(c * CHUNK, (c + 1) * CHUNK)

    def term_step(rows, c):
        term[rows, lanes_of(c)] = lax.dot_general(
            grads[rows, :], wts[lanes_of(c), :], (((1,), (1,)), ((), ())), preferred_element_type=F32
        )

    for by in (1, -1, 2, -2):
        for core in range(2):
            hidden_sent[by, core].wait_recv()
    for j in range(3):
        gate_step(NEAR, j)
    for way in range(2):
        now_2[way, 0].wait_recv()
    send_hidden(4)
    now_3 = now_hop(3, None)
    old_0 = old_hop(0, None)
    for c in range(CHUNKS):
        term_step(NEAR, c)

    moving = {}

    def push(c, way, hop):
        by = 1 - 2 * way
        lanes = lanes_of(c)
        value = term[place((4 - hop) * by), lanes]
        if (c, way, hop - 1) in moving:
            moving[c, way, hop - 1].wait_recv()
            value = value + (land_r, land_l)[way][hop - 1, :, lanes].astype(F32)
        src = (send_r, send_l)[way].at[hop, :, lanes]
        src[...] = value.astype(BF16)
        at = (way * 4 + hop) * CHUNKS + c
        moving[c, way, hop] = send(
            src,
            (land_r, land_l)[way].at[hop, :, lanes],
            red_ss.at[at],
            red_rs.at[at],
            device(-1 if hop == 3 else 0, by, 0),
        )

    order = (0, 2, 1, 3)

    def long_way(c):
        return 0 if c < CHUNKS // 2 else 1

    def dw_step(i):
        rows = slice(i * 256, (i + 1) * 256)
        value = lax.dot_general(
            rows_old[:, rows], old[...], (((0,), (0,)), ((), ())), preferred_element_type=F32
        ).astype(BF16)
        dw_gate[rows, :] = value[:, 0:WIDTH]
        dw_up[rows, :] = value[:, WIDTH:BOTH]

    arrive(now_2, now_3)
    for copy in now_3.values():
        copy.wait_recv()
    for by in (3, -3, 4):
        for core in range(2):
            hidden_sent[by, core].wait_recv()
    for j in range(3):
        gate_step(FAR, j)
    old_1, old_2 = {}, {}
    for turn in range(PIECES):
        old_1 |= old_hop(1, old_0, [turn])
        for c in order[2 * turn : 2 * turn + 2]:
            term_step(FAR, c)
            push(c, long_way(c), 0)
            push(c, 1 - long_way(c), 1)
    share(-1)
    share(1)
    send_o[...] = term[place(0), :].astype(BF16)
    own = send(send_o, land_o, own_ss.at[0], own_rs.at[0], device(-1, 0, 0))
    for turn in range(PIECES):
        old_2 |= old_hop(2, old_1, [turn])
        for c in order[2 * turn : 2 * turn + 2]:
            push(c, long_way(c), 1)
            push(c, 1 - long_way(c), 2)
    share(-2)
    share(2)
    old_3 = old_hop(3, old_2)
    for c in order:
        push(c, long_way(c), 2)
    for c in order:
        push(c, 1 - long_way(c), 3)
    arrive(old_2, old_3)
    share(-3)
    share(3)
    for copy in old_3.values():
        copy.wait_recv()
    share(4, 0, D // 2)
    share(4, D // 2, D)
    for c in order:
        push(c, long_way(c), 3)
    for copy in siblings:
        copy.wait_recv()
    for i in range(12):
        dw_step(i)

    for copy in sent:
        copy.wait_send()
    table_sent.wait_recv()
    own.wait_recv()
    scale = tab_in[:, TOK : TOK + 1]
    for c in order:
        lanes = lanes_of(c)
        moving[c, 0, 3].wait_recv()
        moving[c, 1, 3].wait_recv()
        total = (
            land_o[:, lanes].astype(F32)
            + land_r[3, :, lanes].astype(F32)
            + land_l[3, :, lanes].astype(F32)
        )
        packed_grad[:, lanes] = (scale * total).astype(BF16)


def finish(packed_grad, tab, dw_gate, dw_up, out, out_gate, out_up, spread, sem):
    copies = []
    for src, dst in ((dw_gate, out_gate), (dw_up, out_up)):
        for part in range(2):
            rows = slice(part * (D // 2), (part + 1) * (D // 2))
            copies.append(pltpu.make_async_copy(src.at[rows], dst.at[rows], sem.at[len(copies)]))
            copies[-1].start()
    last = lax.axis_index("section") == lax.axis_size("section") - 1
    back = tab[:, 0:TOK].astype(BF16)
    for c in range(2):
        lanes = slice(c * (D // 2), (c + 1) * (D // 2))
        value = lax.dot_general(
            back, packed_grad[:, lanes], (((0,), (0,)), ((), ())), preferred_element_type=F32
        )
        spread[:, lanes] = jnp.where(last, 0.0, value).astype(BF16)
        copies.append(pltpu.make_async_copy(spread.at[:, lanes], out.at[:, lanes], sem.at[4 + c]))
        copies[-1].start()
    for copy in copies:
        copy.wait()


def shards(
    x_now, ids_now, gates_now, hidden_now, x_old, ids_old, gate_grad_old, up_grad_old, w_gate, w_up
):
    anywhere = pl.BlockSpec(memory_space=pl.ANY)
    dma = pltpu.SemaphoreType.DMA
    inputs = [
        ids_now[0].T, gates_now[0].T, ids_old[0].T, x_now[0], hidden_now[0], x_old[0],
        gate_grad_old[0], up_grad_old[0], w_gate[0], w_up[0],
    ]
    inputs = [pltpu.with_memory_space_constraint(array, pltpu.HBM) for array in inputs]
    packed_grad, tab, dw_gate, dw_up = pl.pallas_call(
        kernel,
        out_shape=(
            pltpu.VMEM((CAP, D), BF16),
            pltpu.VMEM((CAP, 2 * TOK), F32),
            pltpu.VMEM((D, WIDTH), BF16),
            pltpu.VMEM((D, WIDTH), BF16),
        ),
        in_specs=[anywhere] * 10,
        out_specs=[pl.BlockSpec(memory_space=pltpu.VMEM)] * 4,
        scratch_shapes=[
            pltpu.VMEM((4, TOK), jnp.int32),
            pltpu.VMEM((4, TOK), F32),
            pltpu.VMEM((4, TOK), jnp.int32),
            pltpu.VMEM((TOK, D), BF16),
            pltpu.VMEM((TOK, D), BF16),
            pltpu.VMEM((LANE, BOTH), BF16),
            pltpu.VMEM((2 * LANE, BOTH), BF16),
            pltpu.VMEM((D, 2 * BOTH), BF16),
            pltpu.VMEM((LANE, D), BF16),
            pltpu.VMEM((2 * LANE, D), BF16),
            pltpu.VMEM((LANE, 2 * BOTH), BF16),
            pltpu.VMEM((LANE, D), F32),
            pltpu.VMEM((4, CAP, D), BF16),
            pltpu.VMEM((4, CAP, D), BF16),
            pltpu.VMEM((CAP, D), BF16),
            pltpu.VMEM((4, CAP, D), BF16),
            pltpu.VMEM((4, CAP, D), BF16),
            pltpu.VMEM((CAP, D), BF16),
            pltpu.VMEM((CAP, 2 * TOK), F32),
            dma((11,)),
            dma((8 * PIECES,)),
            dma((8 * PIECES,)),
            dma((8 * PIECES,)),
            dma((8 * PIECES,)),
            dma((9,)),
            dma((9,)),
            dma((14,)),
            dma((14,)),
            dma((2,)),
            dma((2,)),
            dma((1,)),
            dma((1,)),
            dma((8 * CHUNKS,)),
            dma((8 * CHUNKS,)),
            dma((1,)),
            dma((1,)),
        ],
        compiler_params=pltpu.CompilerParams(
            collective_id=0, has_side_effects=True, vmem_limit_bytes=48 << 20
        ),
        cost_estimate=pl.CostEstimate(
            flops=3 * 2 * 512 * D * BOTH, bytes_accessed=16 << 20, transcendentals=512 * WIDTH
        ),
    )(*inputs)
    out, dw_gate, dw_up = pl.pallas_call(
        finish,
        out_shape=(
            jax.ShapeDtypeStruct((TOK, D), BF16),
            jax.ShapeDtypeStruct((D, WIDTH), BF16),
            jax.ShapeDtypeStruct((D, WIDTH), BF16),
        ),
        in_specs=[pl.BlockSpec(memory_space=pltpu.VMEM)] * 4,
        out_specs=[pl.BlockSpec(memory_space=pltpu.HBM)] * 3,
        scratch_shapes=[pltpu.VMEM((TOK, D), BF16), dma((6,))],
        compiler_params=pltpu.CompilerParams(vmem_limit_bytes=16 << 20),
    )(packed_grad, tab, dw_gate, dw_up)
    return out[None], dw_gate[None], dw_up[None]


def solution(mesh):
    in_specs = (
        P("section", ("expert", "dp"), None),
        P("section", ("expert", "dp"), None),
        P("section", ("expert", "dp"), None),
        P("section", ("expert", "dp"), None),
        P("section", ("expert", "dp"), None),
        P("section", ("expert", "dp"), None),
        P("section", None, ("expert", "dp")),
        P("section", None, ("expert", "dp")),
        P("section", None, ("expert", "dp")),
        P("section", None, ("expert", "dp")),
    )
    out_specs = (
        P("section", ("expert", "dp"), None),
        P("section", None, ("expert", "dp")),
        P("section", None, ("expert", "dp")),
    )
    return jax.shard_map(shards, mesh=mesh, in_specs=in_specs, out_specs=out_specs, check_vma=False)
```

```python
import jax
import jax.numpy as jnp
from jax import lax
from jax.experimental import pallas as pl
from jax.experimental.pallas import tpu as pltpu
from jax.sharding import PartitionSpec as P

EXPERTS = 16
RING = 8
CAP = 32
TOK = 128
D = 3072
WIDTH = 384
BOTH = 2 * WIDTH
LANE = RING * CAP
PIECES = 2
PIECE = D // PIECES
CHUNKS = 4
CHUNK = D // CHUNKS
ORDER = (0, -1, 1, -2, 2, -3, 3, 4)
NEAR, FAR = slice(0, 5 * CAP), slice(5 * CAP, LANE)
MESH = pl.DeviceIdType.MESH
F32 = jnp.float32
BF16 = jnp.bfloat16


def routing(ids, expert):
    hits = (ids == expert).astype(F32)
    routed = jnp.sum(hits, axis=0, keepdims=True)
    earlier = lax.broadcasted_iota(jnp.int32, (TOK, TOK), 0) < lax.broadcasted_iota(
        jnp.int32, (TOK, TOK), 1
    )
    counts = jnp.dot(
        jnp.broadcast_to(routed, (16, TOK)).astype(BF16),
        earlier.astype(F32).astype(BF16),
        preferred_element_type=F32,
    )
    slot = counts[0:1].astype(jnp.int32)
    places = lax.broadcasted_iota(jnp.int32, (CAP, TOK), 0)
    table = jnp.where((slot == places) & (routed == 1.0), 1.0, 0.0)
    return table, hits


def kernel(
    ids_now, gates_now, ids_old, x_now, hidden, x_old, gate_old, up_old, w_gate, w_up,
    packed_grad, tab_in, dw_gate, dw_up,
    ids_now_v, gates_now_v, ids_old_v, x_now_v, x_old_v, hid, old, wts, rows_now, rows_old,
    grads, term, send_r, send_l, send_o, land_r, land_l, land_o, tab_out,
    load_sem, now_ss, now_rs, old_ss, old_rs, sib_ss, sib_rs, hid_ss, hid_rs, w_ss, w_rs,
    tab_ss, tab_rs, red_ss, red_rs, own_ss, own_rs,
):
    sections = lax.axis_size("section")
    s = lax.axis_index("section")
    e = lax.axis_index("expert")
    z = lax.axis_index("dp") * 2 + e // 2
    k = lax.rem(e, 2)
    expert = lax.rem(s, EXPERTS)

    def chip(by):
        return lax.rem(z + (by + RING), RING)

    def device(by_section, by_z, by_core):
        there = chip(by_z)
        return (
            lax.rem(s + (by_section + sections), sections),
            lax.rem(there, 2) * 2 + lax.rem(k + by_core, 2),
            there // 2,
        )

    def group(there, core):
        return (lax.rem(there, 2) * 2 + core) * 4 + there // 2

    sent = []

    def send(src, dst, ss, rs, to):
        copy = pltpu.make_async_remote_copy(
            src_ref=src, dst_ref=dst, send_sem=ss, recv_sem=rs, device_id=to, device_id_type=MESH
        )
        copy.start()
        sent.append(copy)
        return copy

    barrier = pltpu.get_barrier_semaphore()
    partners = [device(0, 1, 0), device(0, -1, 0), device(0, 0, 1), device(1, 0, 0)]
    for partner in partners:
        pl.semaphore_signal(barrier, inc=1, device_id=partner, device_id_type=MESH)

    loads = 0

    def load(src, dst):
        nonlocal loads
        copy = pltpu.make_async_copy(src, dst, load_sem.at[loads])
        copy.start()
        loads += 1
        return copy

    def columns(start, size, step=128):
        return pl.ds(pl.multiple_of(start, step), size)

    def place(by):
        at = ORDER.index((by + 3) % RING - 3) * CAP
        return slice(at, at + CAP)

    get_now = [load(ids_now, ids_now_v), load(gates_now, gates_now_v), load(x_now, x_now_v)]
    for copy in get_now:
        copy.wait()
    get_old = [load(ids_old, ids_old_v), load(x_old, x_old_v)]
    gate_place, up_place = columns(k * WIDTH, WIDTH), columns(BOTH + k * WIDTH, WIDTH)
    get_weights = [load(w_gate, wts.at[:, gate_place]), load(w_up, wts.at[:, up_place])]
    get_hidden = [
        load(
            hidden.at[:, columns(group(z, core) * WIDTH, WIDTH)],
            hid.at[place(0), core * WIDTH : (core + 1) * WIDTH],
        )
        for core in range(2)
    ]
    get_stored = [load(gate_old, old.at[:, 0:WIDTH]), load(up_old, old.at[:, WIDTH:BOTH])]

    table, hits = routing(ids_now_v[...], expert)
    rows_now[place(0), :] = jnp.dot(
        table.astype(BF16), x_now_v[...], preferred_element_type=F32
    ).astype(BF16)
    weight = jnp.sum(gates_now_v[...] * hits, axis=0, keepdims=True)
    coef = jnp.sum(table * weight, axis=1, keepdims=True)
    tab_out[:, 0:TOK] = table
    tab_out[:, TOK : 2 * TOK] = jnp.broadcast_to(coef, (CAP, TOK))

    pl.semaphore_wait(barrier, len(partners))

    def gather_hop(buf, src, dst, ss, rs, hop, waits, turns):
        copies = {}
        for turn in turns:
            if hop == 3 and turn >= PIECES // 2:
                continue
            for way, by in enumerate((1, -1)):
                if waits is not None:
                    waits[way, turn].wait_recv()
                piece = turn if way == 0 else PIECES - 1 - turn
                lanes = slice(piece * PIECE, (piece + 1) * PIECE)
                at = (way * 4 + hop) * PIECES + turn
                copies[way, turn] = send(
                    buf.at[src(hop, by), lanes],
                    buf.at[dst(hop, by), lanes],
                    ss.at[at],
                    rs.at[at],
                    device(0, by, 0),
                )
        return copies

    def now_hop(hop, waits, turns=range(PIECES)):
        def src(hop, by):
            return place(-hop * by)

        def dst(hop, by):
            return place(-(hop + 1) * by)

        return gather_hop(rows_now, src, dst, now_ss, now_rs, hop, waits, turns)

    def old_place(there):
        return pl.ds(pl.multiple_of(group(there, k) * CAP, CAP), CAP)

    def old_hop(hop, waits, turns=range(PIECES)):
        def both(hop, by):
            return old_place(chip(-hop * by))

        return gather_hop(rows_old, both, both, old_ss, old_rs, hop, waits, turns)

    def arrive(before, after):
        for key, copy in before.items():
            if key not in after:
                copy.wait_recv()

    siblings = []

    def share(by, first=0, last=D):
        block = rows_old.at[old_place(chip(by)), first:last]
        at = len(siblings)
        siblings.append(send(block, block, sib_ss.at[at], sib_rs.at[at], device(0, 0, 1)))

    hidden_sent = {}

    def send_hidden(by):
        there = chip(by)
        for core in range(2):
            at = (by % RING - 1) * 2 + core
            hidden_sent[by, core] = send(
                hidden.at[:, columns(group(there, core) * WIDTH, WIDTH)],
                hid.at[place(-by), core * WIDTH : (core + 1) * WIDTH],
                hid_ss.at[at],
                hid_rs.at[at],
                device(0, by, 0),
            )

    now_0 = now_hop(0, None)
    weights_sent = [
        send(w_gate, wts.at[:, gate_place], w_ss.at[0], w_rs.at[0], device(0, 0, 1)),
        send(w_up, wts.at[:, up_place], w_ss.at[1], w_rs.at[1], device(0, 0, 1)),
    ]
    for by in (1, -1):
        send_hidden(by)
    table_sent = send(tab_out, tab_in, tab_ss.at[0], tab_rs.at[0], device(-1, 0, 0))

    for copy in get_old:
        copy.wait()
    old_table, _ = routing(ids_old_v[...], expert)
    rows_old[old_place(z), :] = jnp.dot(
        old_table.astype(BF16), x_old_v[...], preferred_element_type=F32
    ).astype(BF16)

    share(0)
    now_1 = now_hop(1, now_0)
    for by in (2, -2):
        send_hidden(by)
    now_2 = now_hop(2, now_1)
    for by in (3, -3):
        send_hidden(by)

    for copy in get_weights + get_hidden + get_stored:
        copy.wait()
    for copy in weights_sent:
        copy.wait_recv()

    def gate_step(rows, j):
        lanes = slice(j * 256, (j + 1) * 256)
        up_lanes = slice(BOTH + j * 256, BOTH + (j + 1) * 256)
        gate = jnp.dot(rows_now[rows, :], wts[:, lanes], preferred_element_type=F32)
        up = jnp.dot(rows_now[rows, :], wts[:, up_lanes], preferred_element_type=F32)
        incoming = hid[rows, lanes].astype(F32)
        sig = 1.0 / (1.0 + jnp.exp(-gate))
        act = gate * sig
        slope = sig * (1.0 + gate * (1.0 - sig))
        grads[rows, lanes] = (incoming * up * slope).astype(BF16)
        grads[rows, up_lanes] = (incoming * act).astype(BF16)

    def lanes_of(c):
        return slice(c * CHUNK, (c + 1) * CHUNK)

    def term_step(rows, c):
        term[rows, lanes_of(c)] = lax.dot_general(
            grads[rows, :], wts[lanes_of(c), :], (((1,), (1,)), ((), ())), preferred_element_type=F32
        )

    for by in (1, -1, 2, -2):
        for core in range(2):
            hidden_sent[by, core].wait_recv()
    for j in range(3):
        gate_step(NEAR, j)
    for way in range(2):
        now_2[way, 0].wait_recv()
    send_hidden(4)
    now_3 = now_hop(3, None)
    old_0 = old_hop(0, None)
    for c in range(CHUNKS):
        term_step(NEAR, c)

    moving = {}

    def push(c, way, hop):
        by = 1 - 2 * way
        lanes = lanes_of(c)
        value = term[place((4 - hop) * by), lanes]
        if (c, way, hop - 1) in moving:
            moving[c, way, hop - 1].wait_recv()
            value = value + (land_r, land_l)[way][hop - 1, :, lanes].astype(F32)
        src = (send_r, send_l)[way].at[hop, :, lanes]
        src[...] = value.astype(BF16)
        at = (way * 4 + hop) * CHUNKS + c
        moving[c, way, hop] = send(
            src,
            (land_r, land_l)[way].at[hop, :, lanes],
            red_ss.at[at],
            red_rs.at[at],
            device(-1 if hop == 3 else 0, by, 0),
        )

    order = (0, 2, 1, 3)

    def long_way(c):
        return 0 if c < CHUNKS // 2 else 1

    def dw_step(i):
        rows = slice(i * 256, (i + 1) * 256)
        value = lax.dot_general(
            rows_old[:, rows], old[...], (((0,), (0,)), ((), ())), preferred_element_type=F32
        ).astype(BF16)
        dw_gate[rows, :] = value[:, 0:WIDTH]
        dw_up[rows, :] = value[:, WIDTH:BOTH]

    arrive(now_2, now_3)
    for copy in now_3.values():
        copy.wait_recv()
    for by in (3, -3, 4):
        for core in range(2):
            hidden_sent[by, core].wait_recv()
    for j in range(3):
        gate_step(FAR, j)
    old_1, old_2 = {}, {}
    for turn in range(PIECES):
        old_1 |= old_hop(1, old_0, [turn])
        for c in order[2 * turn : 2 * turn + 2]:
            term_step(FAR, c)
            push(c, long_way(c), 0)
            push(c, 1 - long_way(c), 1)
    share(-1)
    share(1)
    send_o[...] = term[place(0), :].astype(BF16)
    own = send(send_o, land_o, own_ss.at[0], own_rs.at[0], device(-1, 0, 0))
    def reduce_long(turn, hop):
        for c in order[2 * turn : 2 * turn + 2]:
            push(c, long_way(c), hop)

    def reduce_short(turn, hop):
        for c in order[2 * turn : 2 * turn + 2]:
            push(c, 1 - long_way(c), hop)

    old_2 |= old_hop(2, old_1, [0])
    reduce_short(0, 2)
    reduce_long(0, 1)
    old_2 |= old_hop(2, old_1, [1])
    reduce_short(1, 2)
    reduce_long(1, 1)
    share(-2)
    share(2)
    reduce_short(0, 3)
    old_3 = old_hop(3, old_2)
    reduce_long(0, 2)
    reduce_short(1, 3)
    reduce_long(1, 2)
    arrive(old_2, old_3)
    share(-3)
    share(3)
    for copy in old_3.values():
        copy.wait_recv()
    share(4, 0, D // 2)
    share(4, D // 2, D)
    reduce_long(0, 3)
    reduce_long(1, 3)
    for copy in siblings:
        copy.wait_recv()
    for i in range(12):
        dw_step(i)

    for copy in sent:
        copy.wait_send()
    table_sent.wait_recv()
    own.wait_recv()
    scale = tab_in[:, TOK : TOK + 1]
    for c in order:
        lanes = lanes_of(c)
        moving[c, 0, 3].wait_recv()
        moving[c, 1, 3].wait_recv()
        total = (
            land_o[:, lanes].astype(F32)
            + land_r[3, :, lanes].astype(F32)
            + land_l[3, :, lanes].astype(F32)
        )
        packed_grad[:, lanes] = (scale * total).astype(BF16)


def finish(packed_grad, tab, dw_gate, dw_up, out, out_gate, out_up, spread, sem):
    copies = []
    for src, dst in ((dw_gate, out_gate), (dw_up, out_up)):
        for part in range(2):
            rows = slice(part * (D // 2), (part + 1) * (D // 2))
            copies.append(pltpu.make_async_copy(src.at[rows], dst.at[rows], sem.at[len(copies)]))
            copies[-1].start()
    last = lax.axis_index("section") == lax.axis_size("section") - 1
    back = tab[:, 0:TOK].astype(BF16)
    for c in range(2):
        lanes = slice(c * (D // 2), (c + 1) * (D // 2))
        value = lax.dot_general(
            back, packed_grad[:, lanes], (((0,), (0,)), ((), ())), preferred_element_type=F32
        )
        spread[:, lanes] = jnp.where(last, 0.0, value).astype(BF16)
        copies.append(pltpu.make_async_copy(spread.at[:, lanes], out.at[:, lanes], sem.at[4 + c]))
        copies[-1].start()
    for copy in copies:
        copy.wait()


def shards(
    x_now, ids_now, gates_now, hidden_now, x_old, ids_old, gate_grad_old, up_grad_old, w_gate, w_up
):
    anywhere = pl.BlockSpec(memory_space=pl.ANY)
    dma = pltpu.SemaphoreType.DMA
    inputs = [
        ids_now[0].T, gates_now[0].T, ids_old[0].T, x_now[0], hidden_now[0], x_old[0],
        gate_grad_old[0], up_grad_old[0], w_gate[0], w_up[0],
    ]
    inputs = [pltpu.with_memory_space_constraint(array, pltpu.HBM) for array in inputs]
    packed_grad, tab, dw_gate, dw_up = pl.pallas_call(
        kernel,
        out_shape=(
            pltpu.VMEM((CAP, D), BF16),
            pltpu.VMEM((CAP, 2 * TOK), F32),
            pltpu.VMEM((D, WIDTH), BF16),
            pltpu.VMEM((D, WIDTH), BF16),
        ),
        in_specs=[anywhere] * 10,
        out_specs=[pl.BlockSpec(memory_space=pltpu.VMEM)] * 4,
        scratch_shapes=[
            pltpu.VMEM((4, TOK), jnp.int32),
            pltpu.VMEM((4, TOK), F32),
            pltpu.VMEM((4, TOK), jnp.int32),
            pltpu.VMEM((TOK, D), BF16),
            pltpu.VMEM((TOK, D), BF16),
            pltpu.VMEM((LANE, BOTH), BF16),
            pltpu.VMEM((2 * LANE, BOTH), BF16),
            pltpu.VMEM((D, 2 * BOTH), BF16),
            pltpu.VMEM((LANE, D), BF16),
            pltpu.VMEM((2 * LANE, D), BF16),
            pltpu.VMEM((LANE, 2 * BOTH), BF16),
            pltpu.VMEM((LANE, D), F32),
            pltpu.VMEM((4, CAP, D), BF16),
            pltpu.VMEM((4, CAP, D), BF16),
            pltpu.VMEM((CAP, D), BF16),
            pltpu.VMEM((4, CAP, D), BF16),
            pltpu.VMEM((4, CAP, D), BF16),
            pltpu.VMEM((CAP, D), BF16),
            pltpu.VMEM((CAP, 2 * TOK), F32),
            dma((11,)),
            dma((8 * PIECES,)),
            dma((8 * PIECES,)),
            dma((8 * PIECES,)),
            dma((8 * PIECES,)),
            dma((9,)),
            dma((9,)),
            dma((14,)),
            dma((14,)),
            dma((2,)),
            dma((2,)),
            dma((1,)),
            dma((1,)),
            dma((8 * CHUNKS,)),
            dma((8 * CHUNKS,)),
            dma((1,)),
            dma((1,)),
        ],
        compiler_params=pltpu.CompilerParams(
            collective_id=0, has_side_effects=True, vmem_limit_bytes=48 << 20
        ),
        cost_estimate=pl.CostEstimate(
            flops=3 * 2 * 512 * D * BOTH, bytes_accessed=16 << 20, transcendentals=512 * WIDTH
        ),
    )(*inputs)
    out, dw_gate, dw_up = pl.pallas_call(
        finish,
        out_shape=(
            jax.ShapeDtypeStruct((TOK, D), BF16),
            jax.ShapeDtypeStruct((D, WIDTH), BF16),
            jax.ShapeDtypeStruct((D, WIDTH), BF16),
        ),
        in_specs=[pl.BlockSpec(memory_space=pltpu.VMEM)] * 4,
        out_specs=[pl.BlockSpec(memory_space=pltpu.HBM)] * 3,
        scratch_shapes=[pltpu.VMEM((TOK, D), BF16), dma((6,))],
        compiler_params=pltpu.CompilerParams(vmem_limit_bytes=16 << 20),
    )(packed_grad, tab, dw_gate, dw_up)
    return out[None], dw_gate[None], dw_up[None]


def solution(mesh):
    in_specs = (
        P("section", ("expert", "dp"), None),
        P("section", ("expert", "dp"), None),
        P("section", ("expert", "dp"), None),
        P("section", ("expert", "dp"), None),
        P("section", ("expert", "dp"), None),
        P("section", ("expert", "dp"), None),
        P("section", None, ("expert", "dp")),
        P("section", None, ("expert", "dp")),
        P("section", None, ("expert", "dp")),
        P("section", None, ("expert", "dp")),
    )
    out_specs = (
        P("section", ("expert", "dp"), None),
        P("section", None, ("expert", "dp")),
        P("section", None, ("expert", "dp")),
    )
    return jax.shard_map(shards, mesh=mesh, in_specs=in_specs, out_specs=out_specs, check_vma=False)
```
